32 devices in a mesh: panel: 8 (over z, y), chan: 4 (over x, core).
Axes of the slice: x: 2, y: 2, z: 4, core: 2. Of those that a mesh axis runs over, the one named last changes fastest.
Arguments:
- wavefunction: bfloat16 [4, 8, 768, 768], P('chan', 'panel'), may hold values from -6 to 6
- left_env: bfloat16 [2, 8, 768, 768], P(None, 'panel'), may hold values from -0.21875 to 0.21875
- right_env: bfloat16 [2, 8, 768, 768], P(None, 'panel'), may hold values from -0.21875 to 0.21875
- coupling: float32 [2, 4, 4], replicated, may hold values from -4 to 4
- sec_size: int32 [8], replicated, may hold values from 384 to 768, as said below
Outputs:
- applied: bfloat16 [4, 8, 768, 768], P('chan', 'panel')
The draws below stay inside these ranges and needn't reach their ends.
Inputs may be any that keep to these rules, and one draw needn't show every extreme that they name: `sec_size`: sector sizes; some sector holds exactly 768 states.
All inputs are finite; a program needn't handle non-finite values.
Results may differ from the reference program's by a relative error of at most 0.008.
Values may be sent and summed in bfloat16 or wider, within the bound.
A program may use at most 128 MiB of HBM per device.

```python
import jax
import jax.numpy as jnp
from jax import lax

M = 768
PAIRS = 4
CHANNELS = 2
NSEC = 8


def draw_sec_size(key, part):
    values = jax.random.randint(jax.random.fold_in(key, 11), (NSEC,), M // 2, M + 1, dtype=jnp.int32)
    chosen = jax.random.randint(jax.random.fold_in(key, 12), (), 0, NSEC, dtype=jnp.int32)
    slot_ids = jnp.arange(NSEC, dtype=jnp.int32)
    return jnp.where(slot_ids == chosen, M, values).astype(jnp.int32)


def block_scale(key, shape, shards, smallest, largest):
    factor_of = 1.0
    for axis_at, parts in shards:
        heights = jax.random.uniform(jax.random.fold_in(jax.random.fold_in(key, 6), axis_at), (parts,), jnp.float32, smallest / len(shards), largest / len(shards))
        factor_of = factor_of * jnp.repeat(jnp.exp(heights), shape[axis_at] // parts).reshape((-1,) + (1,) * (len(shape) - 1 - axis_at))
    return factor_of


def normal_values(stream_key, extent, scale, bound, shards=(), held_as=jnp.bfloat16):
    values = jax.random.normal(stream_key, extent, jnp.float32) * scale
    if len(shards) > 0:
        values = block_scale(stream_key, extent, shards, -0.22, 0.18) * values
    return jnp.clip(values, min=-bound, max=bound).astype(held_as)


def setup_inputs(seed: int = 0) -> dict:
    streams_of = jax.random.split(jax.random.key(seed), 6)
    wavefunction = normal_values(streams_of[0], (PAIRS, NSEC, M, M), 1.0, 6.0, ((0, 4), (1, 8)))
    left_env = normal_values(streams_of[1], (CHANNELS, NSEC, M, M), M ** -0.5, 0.21875, ((1, 8),))
    right_env = normal_values(streams_of[2], (CHANNELS, NSEC, M, M), M ** -0.5, 0.21875, ((1, 8),))
    coupling = normal_values(streams_of[3], (CHANNELS, PAIRS, PAIRS), 1.0, 4.0, (), jnp.float32)
    sec_size = draw_sec_size(jax.random.fold_in(streams_of[5], 71), 0)
    return {"wavefunction": wavefunction, "left_env": left_env, "right_env": right_env, "coupling": coupling, "sec_size": sec_size}


CHARGE_TABLE = (0, 1, 1, 2)


def outer_dot(left_matrix, right_matrix):
    return lax.dot_general(left_matrix, right_matrix, (((1,), (1,)), ((), ())), preferred_element_type=jnp.float32)


def coupling_masks(coupling):
    charges = jnp.array(CHARGE_TABLE, jnp.int32)
    same_charge = charges[:, None] == charges[None, :]
    raised_charge = charges[None, :] == charges[:, None] + 1
    return jnp.where(same_charge, coupling[0], 0.0), jnp.where(raised_charge, coupling[1], 0.0)


def reference(wavefunction, left_env, right_env, coupling, sec_size):
    same_coef, raise_coef = coupling_masks(coupling)
    positions = jnp.arange(M, dtype=jnp.int32)

    def block_mask(sector, charge_value):
        target = sector + charge_value
        exists = jnp.logical_and(target < NSEC, sector >= 0)
        rows_live = sec_size[jnp.clip(sector, 0, NSEC - 1)]
        cols_live = sec_size[jnp.clip(target, 0, NSEC - 1)]
        row_ok = positions[:, None] < rows_live
        col_ok = positions[None, :] < cols_live
        return jnp.logical_and(jnp.logical_and(row_ok, col_ok), exists)

    def right_block(channel, target):
        clipped = jnp.clip(target, 0, NSEC - 1).astype(jnp.int32)
        found = right_env[channel, clipped]
        inside = jnp.logical_and(target >= 0, target < NSEC)
        return jnp.where(inside, found, jnp.zeros_like(found))

    def one_sector(sector):
        previous = jnp.maximum(sector - 1, 0)
        summed = jnp.zeros((PAIRS, M, M), jnp.float32)
        for source in range(PAIRS):
            charge_value = CHARGE_TABLE[source]
            here_block = wavefunction[source, sector]
            here = jnp.where(block_mask(sector, charge_value), here_block, jnp.zeros_like(here_block))
            lower_block = wavefunction[source, previous]
            lower_ok = jnp.logical_and(block_mask(sector - 1, charge_value), sector >= 1)
            lower = jnp.where(lower_ok, lower_block, jnp.zeros_like(lower_block))
            same_sector = jnp.dot(left_env[0, sector], here, preferred_element_type=jnp.float32).astype(jnp.bfloat16)
            raised = jnp.dot(left_env[1, sector], lower, preferred_element_type=jnp.float32).astype(jnp.bfloat16)
            kept_terms = outer_dot(same_sector, right_block(0, sector + charge_value))
            moved_terms = outer_dot(raised, right_block(1, sector - 1 + charge_value))
            summed = summed + same_coef[:, source][:, None, None] * kept_terms[None] + raise_coef[:, source][:, None, None] * moved_terms[None]
        masks = jnp.stack([block_mask(sector, CHARGE_TABLE[target_pair]) for target_pair in range(PAIRS)])
        return jnp.where(masks, summed, 0.0).astype(jnp.bfloat16)

    result = lax.map(one_sector, jnp.arange(NSEC, dtype=jnp.int32))
    return jnp.transpose(result, (1, 0, 2, 3))
```

```python
import functools

import jax
import jax.numpy as jnp
from jax import lax
from jax.experimental import pallas as pl
from jax.experimental.pallas import tpu as pltpu
from jax.sharding import PartitionSpec as P

MESH = pl.DeviceIdType.MESH
STEP = 128
ROWS = 256
BF16 = jnp.bfloat16


def dot(a, b):
    return jnp.dot(a, b, preferred_element_type=jnp.float32)


def outer_dot(a, b):
    return lax.dot_general(a, b, (((1,), (1,)), ((), ())), preferred_element_type=jnp.float32)


def inside(shape, row0, col0, rows_live, cols_live):
    row = lax.broadcasted_iota(jnp.int32, shape, 0) + row0
    col = lax.broadcasted_iota(jnp.int32, shape, 1) + col0
    return jnp.logical_and(row < rows_live, col < cols_live)


def kernel(
    sectors,
    coupling,
    sec_size,
    psi_hbm,
    left_hbm,
    right_hbm,
    out,
    left,
    right,
    own,
    in_psi,
    in_right,
    in_part,
    out_part,
    mix_a,
    mix_b,
    mix_c,
    half_a,
    half_b,
    acc,
    local_sem,
    psi_send,
    psi_recv,
    right_send,
    right_recv,
    part_send,
    part_recv,
):
    width = own.shape[0]
    steps = width // STEP
    p = lax.axis_index("panel")
    pair = lax.axis_index("chan")
    last = sectors - 1

    psi_src = psi_hbm.at[0, 0]
    left_copies = [
        pltpu.make_async_copy(left_hbm.at[k, 0], left.at[k], local_sem.at[k]) for k in range(2)
    ]
    right_copies = [
        pltpu.make_async_copy(right_hbm.at[k, 0], right.at[k], local_sem.at[2 + k])
        for k in range(2)
    ]
    own_copy = pltpu.make_async_copy(psi_src, own, local_sem.at[4])

    def live(sector):
        exists = jnp.logical_and(sector >= 0, sector < sectors)
        return jnp.where(exists, sec_size[jnp.clip(sector, 0, last)], 0)

    def rows_at(ref, c, n=STEP):
        return ref.at[pl.ds(pl.multiple_of(c * n, n), n), :]

    def remote(src, dst, send, recv, panel, chan):
        return pltpu.make_async_remote_copy(
            src_ref=src,
            dst_ref=dst,
            send_sem=send,
            recv_sem=recv,
            device_id={"panel": panel, "chan": chan},
            device_id_type=MESH,
        )

    def psi_copy(src, c, panel, chan):
        return remote(rows_at(src, c), rows_at(in_psi, c), psi_send.at[c], psi_recv.at[c], panel, chan)

    def right_copy(k, c, panel, chan):
        src = rows_at(right_hbm.at[k, 0], c)
        return remote(src, rows_at(in_right, c), right_send.at[c], right_recv.at[c], panel, chan)

    def part_copy(c, panel, chan):
        return remote(
            out_part.at[c], in_part.at[c], part_send.at[c], part_recv.at[c], panel, chan
        )

    def each(body, n=None):
        def step(c, carry):
            body(c)
            return carry

        lax.fori_loop(0, steps if n is None else n, step, 0)

    def multiply(dst, a, b):
        def body(r):
            at = pl.ds(pl.multiple_of(r * ROWS, ROWS), ROWS)
            dst[at, :] = dot(a[at, :], b[...]).astype(BF16)

        each(body, width // ROWS)

    def mask_block(dst, src, rows_live, cols_live):
        def body(c):
            at = pl.ds(pl.multiple_of(c * STEP, STEP), STEP)
            block = src[at, :]
            keep = inside(block.shape, c * STEP, 0, rows_live, cols_live)
            dst[at, :] = jnp.where(keep, block.astype(jnp.float32), 0.0).astype(BF16)

        each(body)

    def write_out(c, value, rows_live, cols_live):
        at = pl.ds(pl.multiple_of(c * STEP, STEP), STEP)
        keep = inside(value.shape, 0, c * STEP, rows_live, cols_live)
        out[0, 0, :, at] = jnp.where(keep, value, 0.0).astype(BF16)

    def write_zeros():
        out[...] = jnp.zeros_like(out)

    @pl.when(pair != 2)
    def _():
        left_copies[0].start()
        own_copy.start()

    @pl.when(jnp.logical_or(pair == 0, pair == 2))
    def _():
        left_copies[1].start()

    @pl.when(pair == 0)
    def _():
        right_copies[0].start()
        right_copies[1].start()

    barrier = pltpu.get_barrier_semaphore()
    partners = (
        (0, p >= 1, -1, 1),
        (1, p < last, 1, 0),
        (1, p < last, 0, 2),
        (2, p < last, 0, 1),
        (2, jnp.logical_and(p >= 1, p < last), -1, 3),
        (2, p >= 1, -1, 2),
        (2, p < last, 1, 2),
        (3, p < last - 1, 1, 2),
        (3, p < last - 1, 2, 3),
        (3, p >= 2, -2, 3),
    )
    for role, meets, shift, chan in partners:

        @pl.when(jnp.logical_and(pair == role, meets))
        def _(shift=shift, chan=chan):
            pl.semaphore_signal(
                barrier, inc=1, device_id={"panel": p + shift, "chan": chan}, device_id_type=MESH
            )

    met = sum(
        jnp.where(jnp.logical_and(pair == role, meets), 1, 0) for role, meets, _, _ in partners
    )

    @pl.when(met > 0)
    def _():
        pl.semaphore_wait(barrier, met)

    @pl.when(pair == 0)
    def _pair0():
        @pl.when(p >= 1)
        def _():
            each(lambda c: right_copy(0, c, p - 1, 1).start())

        left_copies[0].wait()
        own_copy.wait()
        rows_live, cols_live = live(p), live(p)
        mask_block(own, own, rows_live, cols_live)
        multiply(half_a, left.at[0], own)
        right_copies[0].wait()
        weight = coupling[0, 0, 0]

        def kept(c):
            acc[c] = weight * outer_dot(half_a[...], right[0, pl.ds(pl.multiple_of(c * STEP, STEP), STEP), :])

        each(kept)
        right_copies[1].wait()
        left_copies[1].wait()

        @pl.when(p >= 1)
        def _():
            def fold(c):
                psi_copy(in_psi, c, p - 1, 1).wait_recv()
                at = pl.ds(pl.multiple_of(c * STEP, STEP), STEP)
                half_b[at, :] = outer_dot(in_psi[at, :], right[1]).astype(BF16)

            each(fold)

            def finish(c):
                at = pl.ds(pl.multiple_of(c * STEP, STEP), STEP)
                write_out(c, acc[c] + dot(left[1], half_b[:, at]), rows_live, cols_live)

            each(finish)
            each(lambda c: right_copy(0, c, p - 1, 1).wait_send())

        @pl.when(p == 0)
        def _():
            each(lambda c: write_out(c, acc[c], rows_live, cols_live))

    @pl.when(pair == 1)
    def _pair1():
        left_copies[0].wait()
        own_copy.wait()

        @pl.when(p == last)
        def _():
            write_zeros()

        @pl.when(p < last)
        def _():
            rows_live, cols_live = live(p), live(p + 1)

            def mix(c):
                psi_copy(in_psi, c, p, 2).wait_recv()
                at = pl.ds(pl.multiple_of(c * STEP, STEP), STEP)
                mine = own[at, :].astype(jnp.float32)
                theirs = in_psi[at, :].astype(jnp.float32)
                keep = inside(mine.shape, c * STEP, 0, rows_live, cols_live)

                def blend(x, y):
                    return jnp.where(keep, x * mine + y * theirs, 0.0).astype(BF16)

                mix_a[at, :] = blend(coupling[1, 0, 1], coupling[1, 0, 2])
                psi_copy(mix_a, c, p + 1, 0).start()
                mix_b[at, :] = blend(coupling[0, 1, 1], coupling[0, 1, 2])
                mix_c[at, :] = blend(coupling[0, 2, 1], coupling[0, 2, 2])

            each(mix)
            multiply(half_b, left.at[0], mix_c)
            multiply(half_a, left.at[0], mix_b)

            def kept(c):
                right_copy(0, c, p + 1, 0).wait_recv()
                block = in_right[pl.ds(pl.multiple_of(c * STEP, STEP), STEP), :]
                out_part[c] = outer_dot(half_b[...], block).astype(BF16)
                part_copy(c, p, 2).start()
                acc[c] = outer_dot(half_a[...], block)

            each(kept)

            def finish(c):
                part_copy(c, p, 2).wait_recv()
                moved = coupling[1, 1, 3] * in_part[c].astype(jnp.float32)
                write_out(c, acc[c] + moved, rows_live, cols_live)

            each(finish)
            each(lambda c: psi_copy(mix_a, c, p + 1, 0).wait_send())
            each(lambda c: part_copy(c, p, 2).wait_send())

    @pl.when(pair == 2)
    def _pair2():
        @pl.when(p < last)
        def _():
            each(lambda c: psi_copy(psi_src, c, p, 1).start())

        left_copies[1].wait()

        @pl.when(jnp.logical_and(p >= 1, p < last))
        def _():
            each(lambda c: psi_copy(in_psi, c, p - 1, 3).wait_recv())

        @pl.when(p >= 1)
        def _():
            each(lambda c: right_copy(1, c, p - 1, 2).start())

        @pl.when(p == last)
        def _():
            write_zeros()

        @pl.when(p < last)
        def _():
            rows_live, cols_live = live(p), live(p + 1)

            @pl.when(p >= 1)
            def _():
                mask_block(mix_a, in_psi, live(p - 1), live(p + 1))

            @pl.when(p == 0)
            def _():
                mix_a[...] = jnp.zeros_like(mix_a)

            multiply(half_a, left.at[1], mix_a)

            def moved(c):
                right_copy(1, c, p + 1, 2).wait_recv()
                block = in_right[pl.ds(pl.multiple_of(c * STEP, STEP), STEP), :]
                value = outer_dot(half_a[...], block)
                out_part[c] = value.astype(BF16)
                part_copy(c, p, 1).start()
                acc[c] = coupling[1, 2, 3] * value

            each(moved)

            def finish(c):
                part_copy(c, p, 1).wait_recv()
                write_out(c, acc[c] + in_part[c].astype(jnp.float32), rows_live, cols_live)

            each(finish)
            each(lambda c: psi_copy(psi_src, c, p, 1).wait_send())
            each(lambda c: part_copy(c, p, 1).wait_send())

        @pl.when(p >= 1)
        def _():
            each(lambda c: right_copy(1, c, p - 1, 2).wait_send())

    @pl.when(pair == 3)
    def _pair3():
        @pl.when(p < last - 1)
        def _():
            each(lambda c: psi_copy(psi_src, c, p + 1, 2).start())

        @pl.when(p >= 2)
        def _():
            each(lambda c: right_copy(0, c, p - 2, 3).start())

        left_copies[0].wait()
        own_copy.wait()

        @pl.when(p >= last - 1)
        def _():
            write_zeros()

        @pl.when(p < last - 1)
        def _():
            rows_live, cols_live = live(p), live(p + 2)
            mask_block(own, own, rows_live, cols_live)
            multiply(half_a, left.at[0], own)

            def kept(c):
                right_copy(0, c, p + 2, 3).wait_recv()
                block = in_right[pl.ds(pl.multiple_of(c * STEP, STEP), STEP), :]
                value = coupling[0, 3, 3] * outer_dot(half_a[...], block)
                write_out(c, value, rows_live, cols_live)

            each(kept)
            each(lambda c: psi_copy(psi_src, c, p + 1, 2).wait_send())

        @pl.when(p >= 2)
        def _():
            each(lambda c: right_copy(0, c, p - 2, 3).wait_send())


def shards(sectors, wavefunction, left_env, right_env, coupling, sec_size):
    width = wavefunction.shape[-1]
    steps = width // STEP
    square = pltpu.VMEM((width, width), BF16)
    strips = (steps, width, STEP)
    return pl.pallas_call(
        functools.partial(kernel, sectors),
        out_shape=jax.ShapeDtypeStruct(wavefunction.shape, BF16),
        in_specs=[pl.BlockSpec(memory_space=pltpu.SMEM)] * 2
        + [pl.BlockSpec(memory_space=pl.ANY)] * 3,
        out_specs=pl.BlockSpec(memory_space=pltpu.VMEM),
        scratch_shapes=[
            pltpu.VMEM((2, width, width), BF16),
            pltpu.VMEM((2, width, width), BF16),
            square,
            square,
            square,
            pltpu.VMEM(strips, BF16),
            pltpu.VMEM(strips, BF16),
            square,
            square,
            square,
            square,
            square,
            pltpu.VMEM(strips, jnp.float32),
            pltpu.SemaphoreType.DMA((5,)),
        ]
        + [pltpu.SemaphoreType.DMA((steps,))] * 6,
        compiler_params=pltpu.CompilerParams(
            collective_id=0, has_side_effects=True, vmem_limit_bytes=48 * 1024 * 1024
        ),
    )(coupling, sec_size, wavefunction, left_env, right_env)


def solution(mesh):
    sectors = mesh.shape["panel"]
    return jax.shard_map(
        functools.partial(shards, sectors),
        mesh=mesh,
        in_specs=(
            P("chan", "panel", None, None),
            P(None, "panel", None, None),
            P(None, "panel", None, None),
            P(),
            P(),
        ),
        out_specs=P("chan", "panel", None, None),
        check_vma=False,
    )
```

```python
import functools

import jax
import jax.numpy as jnp
from jax import lax
from jax.experimental import pallas as pl
from jax.experimental.pallas import tpu as pltpu
from jax.sharding import PartitionSpec as P

MESH = pl.DeviceIdType.MESH
STEP = 128
ROWS = 256
BF16 = jnp.bfloat16


def dot(a, b):
    return jnp.dot(a, b, preferred_element_type=jnp.float32)


def outer_dot(a, b):
    return lax.dot_general(a, b, (((1,), (1,)), ((), ())), preferred_element_type=jnp.float32)


def inside(shape, row0, col0, rows_live, cols_live):
    row = lax.broadcasted_iota(jnp.int32, shape, 0) + row0
    col = lax.broadcasted_iota(jnp.int32, shape, 1) + col0
    return jnp.logical_and(row < rows_live, col < cols_live)


def kernel(
    sectors,
    coupling_hbm,
    sec_size_hbm,
    psi_hbm,
    left_hbm,
    right_hbm,
    out,
    left,
    right,
    own,
    in_psi,
    in_right,
    in_part,
    out_part,
    mix_a,
    mix_b,
    mix_c,
    half_a,
    half_b,
    acc,
    coupling,
    sec_size,
    local_sem,
    psi_send,
    psi_recv,
    right_send,
    right_recv,
    part_send,
    part_recv,
):
    width = own.shape[0]
    steps = width // STEP
    early = steps // 2
    p = lax.axis_index("panel")
    pair = lax.axis_index("chan")
    last = sectors - 1

    psi_src = psi_hbm.at[0, 0]
    left_copies = [
        pltpu.make_async_copy(left_hbm.at[k, 0], left.at[k], local_sem.at[k]) for k in range(2)
    ]
    right_copies = [
        pltpu.make_async_copy(right_hbm.at[k, 0], right.at[k], local_sem.at[2 + k])
        for k in range(2)
    ]
    own_copy = pltpu.make_async_copy(psi_src, own, local_sem.at[4])
    coupling_copy = pltpu.make_async_copy(coupling_hbm, coupling, local_sem.at[5])
    size_copy = pltpu.make_async_copy(sec_size_hbm, sec_size, local_sem.at[6])
    coupling_copy.start()
    size_copy.start()

    def live(sector):
        exists = jnp.logical_and(sector >= 0, sector < sectors)
        return jnp.where(exists, sec_size[jnp.clip(sector, 0, last)], 0)

    def rows_at(ref, c, n=STEP):
        return ref.at[pl.ds(pl.multiple_of(c * n, n), n), :]

    def remote(src, dst, send, recv, panel, chan):
        return pltpu.make_async_remote_copy(
            src_ref=src,
            dst_ref=dst,
            send_sem=send,
            recv_sem=recv,
            device_id={"panel": panel, "chan": chan},
            device_id_type=MESH,
        )

    def psi_copy(src, c, panel, chan):
        return remote(rows_at(src, c), rows_at(in_psi, c), psi_send.at[c], psi_recv.at[c], panel, chan)

    def right_copy(k, c, panel, chan):
        src = rows_at(right_hbm.at[k, 0], c)
        return remote(src, rows_at(in_right, c), right_send.at[c], right_recv.at[c], panel, chan)

    def part_copy(c, panel, chan):
        return remote(
            out_part.at[c], in_part.at[c], part_send.at[c], part_recv.at[c], panel, chan
        )

    def each(body, n=None):
        def step(c, carry):
            body(c)
            return carry

        lax.fori_loop(0, steps if n is None else n, step, 0)

    def multiply(dst, a, b):
        def body(r):
            at = pl.ds(pl.multiple_of(r * ROWS, ROWS), ROWS)
            dst[at, :] = dot(a[at, :], b[...]).astype(BF16)

        each(body, width // ROWS)

    def mask_block(dst, src, rows_live, cols_live):
        def body(c):
            at = pl.ds(pl.multiple_of(c * STEP, STEP), STEP)
            block = src[at, :]
            keep = inside(block.shape, c * STEP, 0, rows_live, cols_live)
            dst[at, :] = jnp.where(keep, block.astype(jnp.float32), 0.0).astype(BF16)

        each(body)

    def write_out(c, value, rows_live, cols_live):
        at = pl.ds(pl.multiple_of(c * STEP, STEP), STEP)
        keep = inside(value.shape, 0, c * STEP, rows_live, cols_live)
        out[0, 0, :, at] = jnp.where(keep, value, 0.0).astype(BF16)

    def write_zeros():
        out[...] = jnp.zeros_like(out)

    @pl.when(pair != 2)
    def _():
        left_copies[0].start()
        own_copy.start()

    @pl.when(jnp.logical_or(pair == 0, pair == 2))
    def _():
        left_copies[1].start()

    @pl.when(pair == 0)
    def _():
        right_copies[0].start()
        right_copies[1].start()

    barrier = pltpu.get_barrier_semaphore()
    partners = (
        (0, p >= 1, -1, 1),
        (1, p < last, 1, 0),
        (1, p < last, 0, 2),
        (2, p < last, 0, 1),
        (2, jnp.logical_and(p >= 1, p < last), -1, 3),
        (2, p >= 1, -1, 2),
        (2, p < last, 1, 2),
        (3, p < last - 1, 1, 2),
        (3, p < last - 1, 2, 3),
        (3, p >= 2, -2, 3),
    )
    for role, meets, shift, chan in partners:

        @pl.when(jnp.logical_and(pair == role, meets))
        def _(shift=shift, chan=chan):
            pl.semaphore_signal(
                barrier, inc=1, device_id={"panel": p + shift, "chan": chan}, device_id_type=MESH
            )

    met = sum(
        jnp.where(jnp.logical_and(pair == role, meets), 1, 0) for role, meets, _, _ in partners
    )

    @pl.when(met > 0)
    def _():
        pl.semaphore_wait(barrier, met)

    coupling_copy.wait()
    size_copy.wait()

    @pl.when(pair == 0)
    def _pair0():
        @pl.when(p >= 1)
        def _():
            each(lambda c: right_copy(0, c, p - 1, 1).start())

        left_copies[0].wait()
        own_copy.wait()
        rows_live, cols_live = live(p), live(p)
        mask_block(own, own, rows_live, cols_live)
        multiply(half_a, left.at[0], own)
        right_copies[0].wait()
        weight = coupling[0, 0, 0]

        def kept(c):
            acc[c] = weight * outer_dot(half_a[...], right[0, pl.ds(pl.multiple_of(c * STEP, STEP), STEP), :])

        each(kept)
        right_copies[1].wait()
        left_copies[1].wait()

        @pl.when(p >= 1)
        def _():
            def fold(c):
                psi_copy(in_psi, c, p - 1, 1).wait_recv()
                at = pl.ds(pl.multiple_of(c * STEP, STEP), STEP)
                half_b[at, :] = outer_dot(in_psi[at, :], right[1]).astype(BF16)

            each(fold)

            def finish(c):
                at = pl.ds(pl.multiple_of(c * STEP, STEP), STEP)
                write_out(c, acc[c] + dot(left[1], half_b[:, at]), rows_live, cols_live)

            each(finish)
            each(lambda c: right_copy(0, c, p - 1, 1).wait_send())

        @pl.when(p == 0)
        def _():
            each(lambda c: write_out(c, acc[c], rows_live, cols_live))

    @pl.when(pair == 1)
    def _pair1():
        left_copies[0].wait()
        own_copy.wait()

        @pl.when(p == last)
        def _():
            write_zeros()

        @pl.when(p < last)
        def _():
            rows_live, cols_live = live(p), live(p + 1)

            def mix(c):
                psi_copy(in_psi, c, p, 2).wait_recv()
                at = pl.ds(pl.multiple_of(c * STEP, STEP), STEP)
                mine = own[at, :].astype(jnp.float32)
                theirs = in_psi[at, :].astype(jnp.float32)
                keep = inside(mine.shape, c * STEP, 0, rows_live, cols_live)

                def blend(x, y):
                    return jnp.where(keep, x * mine + y * theirs, 0.0).astype(BF16)

                mix_a[at, :] = blend(coupling[1, 0, 1], coupling[1, 0, 2])
                psi_copy(mix_a, c, p + 1, 0).start()
                mix_b[at, :] = blend(coupling[0, 1, 1], coupling[0, 1, 2])
                mix_c[at, :] = blend(coupling[0, 2, 1], coupling[0, 2, 2])

            each(mix)
            multiply(half_b, left.at[0], mix_c)
            multiply(half_a, left.at[0], mix_b)

            def kept(c):
                right_copy(0, c, p + 1, 0).wait_recv()
                block = in_right[pl.ds(pl.multiple_of(c * STEP, STEP), STEP), :]
                out_part[c] = outer_dot(half_b[...], block).astype(BF16)
                part_copy(c, p, 2).start()
                acc[c] = outer_dot(half_a[...], block)

            each(kept)

            def finish(c):
                part_copy(c, p, 2).wait_recv()
                moved = coupling[1, 1, 3] * in_part[c].astype(jnp.float32)
                write_out(c, acc[c] + moved, rows_live, cols_live)

            each(finish)
            each(lambda c: psi_copy(mix_a, c, p + 1, 0).wait_send())
            each(lambda c: part_copy(c, p, 2).wait_send())

    @pl.when(pair == 2)
    def _pair2():
        @pl.when(p < last)
        def _():
            each(lambda c: psi_copy(psi_src, c, p, 1).start())

        left_copies[1].wait()

        @pl.when(jnp.logical_and(p >= 1, p < last))
        def _():
            each(lambda c: psi_copy(in_psi, c, p - 1, 3).wait_recv(), early)

        @pl.when(p >= 1)
        def _():
            each(lambda c: right_copy(1, c, p - 1, 2).start())

        @pl.when(jnp.logical_and(p >= 1, p < last))
        def _():
            each(lambda c: psi_copy(in_psi, c + early, p - 1, 3).wait_recv(), steps - early)

        @pl.when(p == last)
        def _():
            write_zeros()

        @pl.when(p < last)
        def _():
            rows_live, cols_live = live(p), live(p + 1)

            @pl.when(p >= 1)
            def _():
                mask_block(mix_a, in_psi, live(p - 1), live(p + 1))

            @pl.when(p == 0)
            def _():
                mix_a[...] = jnp.zeros_like(mix_a)

            multiply(half_a, left.at[1], mix_a)

            def moved(c):
                right_copy(1, c, p + 1, 2).wait_recv()
                block = in_right[pl.ds(pl.multiple_of(c * STEP, STEP), STEP), :]
                value = outer_dot(half_a[...], block)
                out_part[c] = value.astype(BF16)
                part_copy(c, p, 1).start()
                acc[c] = coupling[1, 2, 3] * value

            each(moved)

            def finish(c):
                part_copy(c, p, 1).wait_recv()
                write_out(c, acc[c] + in_part[c].astype(jnp.float32), rows_live, cols_live)

            each(finish)
            each(lambda c: psi_copy(psi_src, c, p, 1).wait_send())
            each(lambda c: part_copy(c, p, 1).wait_send())

        @pl.when(p >= 1)
        def _():
            each(lambda c: right_copy(1, c, p - 1, 2).wait_send())

    @pl.when(pair == 3)
    def _pair3():
        @pl.when(p < last - 1)
        def _():
            each(lambda c: psi_copy(psi_src, c, p + 1, 2).start())

        @pl.when(p >= 2)
        def _():
            each(lambda c: right_copy(0, c, p - 2, 3).start())

        left_copies[0].wait()
        own_copy.wait()

        @pl.when(p >= last - 1)
        def _():
            write_zeros()

        @pl.when(p < last - 1)
        def _():
            rows_live, cols_live = live(p), live(p + 2)
            mask_block(own, own, rows_live, cols_live)
            multiply(half_a, left.at[0], own)

            def kept(c):
                right_copy(0, c, p + 2, 3).wait_recv()
                block = in_right[pl.ds(pl.multiple_of(c * STEP, STEP), STEP), :]
                value = coupling[0, 3, 3] * outer_dot(half_a[...], block)
                write_out(c, value, rows_live, cols_live)

            each(kept)
            each(lambda c: psi_copy(psi_src, c, p + 1, 2).wait_send())

        @pl.when(p >= 2)
        def _():
            each(lambda c: right_copy(0, c, p - 2, 3).wait_send())


def shards(sectors, wavefunction, left_env, right_env, coupling, sec_size):
    width = wavefunction.shape[-1]
    steps = width // STEP
    square = pltpu.VMEM((width, width), BF16)
    strips = (steps, width, STEP)
    return pl.pallas_call(
        functools.partial(kernel, sectors),
        out_shape=jax.ShapeDtypeStruct(wavefunction.shape, BF16),
        in_specs=[pl.BlockSpec(memory_space=pl.ANY)] * 5,
        out_specs=pl.BlockSpec(memory_space=pltpu.VMEM),
        scratch_shapes=[
            pltpu.VMEM((2, width, width), BF16),
            pltpu.VMEM((2, width, width), BF16),
            square,
            square,
            square,
            pltpu.VMEM(strips, BF16),
            pltpu.VMEM(strips, BF16),
            square,
            square,
            square,
            square,
            square,
            pltpu.VMEM(strips, jnp.float32),
            pltpu.SMEM(coupling.shape, coupling.dtype),
            pltpu.SMEM(sec_size.shape, sec_size.dtype),
            pltpu.SemaphoreType.DMA((7,)),
        ]
        + [pltpu.SemaphoreType.DMA((steps,))] * 6,
        compiler_params=pltpu.CompilerParams(
            collective_id=0, has_side_effects=True, vmem_limit_bytes=56 * 1024 * 1024
        ),
    )(coupling, sec_size, wavefunction, left_env, right_env)


def solution(mesh):
    sectors = mesh.shape["panel"]
    return jax.shard_map(
        functools.partial(shards, sectors),
        mesh=mesh,
        in_specs=(
            P("chan", "panel", None, None),
            P(None, "panel", None, None),
            P(None, "panel", None, None),
            P(),
            P(),
        ),
        out_specs=P("chan", "panel", None, None),
        check_vma=False,
    )
```

```python
import functools

import jax
import jax.numpy as jnp
from jax import lax
from jax.experimental import pallas as pl
from jax.experimental.pallas import tpu as pltpu
from jax.sharding import PartitionSpec as P

MESH = pl.DeviceIdType.MESH
STEP = 128
ROWS = 256
BF16 = jnp.bfloat16


def dot(a, b):
    return jnp.dot(a, b, preferred_element_type=jnp.float32)


def outer_dot(a, b):
    return lax.dot_general(a, b, (((1,), (1,)), ((), ())), preferred_element_type=jnp.float32)


def inside(shape, row0, col0, rows_live, cols_live):
    row = lax.broadcasted_iota(jnp.int32, shape, 0) + row0
    col = lax.broadcasted_iota(jnp.int32, shape, 1) + col0
    return jnp.logical_and(row < rows_live, col < cols_live)


def kernel(
    sectors,
    coupling_hbm,
    sec_size_hbm,
    psi_hbm,
    left_hbm,
    right_hbm,
    out,
    left,
    right,
    own,
    in_psi,
    in_right,
    in_part,
    out_part,
    mixed,
    both,
    half_a,
    half_b,
    acc,
    coupling,
    sec_size,
    local_sem,
    psi_send,
    psi_recv,
    right_send,
    right_recv,
    part_send,
    part_recv,
):
    width = own.shape[0]
    steps = width // STEP
    early = steps // 2
    p = lax.axis_index("panel")
    pair = lax.axis_index("chan")
    last = sectors - 1

    psi_src = psi_hbm.at[0, 0]
    left_copies = [
        pltpu.make_async_copy(left_hbm.at[k, 0], left.at[k], local_sem.at[k]) for k in range(2)
    ]
    right_copies = [
        pltpu.make_async_copy(right_hbm.at[k, 0], right.at[k], local_sem.at[2 + k])
        for k in range(2)
    ]
    own_copy = pltpu.make_async_copy(psi_src, own, local_sem.at[4])
    coupling_copy = pltpu.make_async_copy(coupling_hbm, coupling, local_sem.at[5])
    size_copy = pltpu.make_async_copy(sec_size_hbm, sec_size, local_sem.at[6])
    coupling_copy.start()
    size_copy.start()

    def live(sector):
        exists = jnp.logical_and(sector >= 0, sector < sectors)
        return jnp.where(exists, sec_size[jnp.clip(sector, 0, last)], 0)

    def rows_at(ref, c, n=STEP):
        return ref.at[pl.ds(pl.multiple_of(c * n, n), n), :]

    def remote(src, dst, send, recv, panel, chan):
        return pltpu.make_async_remote_copy(
            src_ref=src,
            dst_ref=dst,
            send_sem=send,
            recv_sem=recv,
            device_id={"panel": panel, "chan": chan},
            device_id_type=MESH,
        )

    def strip(c):
        return pl.ds(pl.multiple_of(c * STEP, STEP), STEP)

    def strip_copy(src, c, panel, chan):
        return remote(src, in_psi.at[c], psi_send.at[c], psi_recv.at[c], panel, chan)

    def psi_copy(c, panel, chan):
        return strip_copy(psi_src.at[:, strip(c)], c, panel, chan)

    def mix_copy(c, panel, chan):
        return strip_copy(mixed.at[c], c, panel, chan)

    def right_copy(k, c, panel, chan):
        src = rows_at(right_hbm.at[k, 0], c)
        return remote(src, rows_at(in_right, c), right_send.at[c], right_recv.at[c], panel, chan)

    def part_copy(c, panel, chan):
        return remote(
            out_part.at[c], in_part.at[c], part_send.at[c], part_recv.at[c], panel, chan
        )

    def each(body, n=None):
        def step(c, carry):
            body(c)
            return carry

        lax.fori_loop(0, steps if n is None else n, step, 0)

    def multiply(dst, a, b):
        def body(r):
            at = pl.ds(pl.multiple_of(r * ROWS, ROWS), ROWS)
            dst[at, :] = dot(a[at, :], b[...]).astype(BF16)

        each(body, width // ROWS)

    def mask_block(dst, src, rows_live, cols_live):
        def body(c):
            at = pl.ds(pl.multiple_of(c * STEP, STEP), STEP)
            block = src[at, :]
            keep = inside(block.shape, c * STEP, 0, rows_live, cols_live)
            dst[at, :] = jnp.where(keep, block.astype(jnp.float32), 0.0).astype(BF16)

        each(body)

    def write_out(c, value, rows_live, cols_live):
        at = pl.ds(pl.multiple_of(c * STEP, STEP), STEP)
        keep = inside(value.shape, 0, c * STEP, rows_live, cols_live)
        out[0, 0, :, at] = jnp.where(keep, value, 0.0).astype(BF16)

    def write_zeros():
        out[...] = jnp.zeros_like(out)

    @pl.when(pair != 2)
    def _():
        left_copies[0].start()
        own_copy.start()

    @pl.when(jnp.logical_or(pair == 0, pair == 2))
    def _():
        left_copies[1].start()

    @pl.when(pair == 0)
    def _():
        right_copies[0].start()
        right_copies[1].start()

    barrier = pltpu.get_barrier_semaphore()
    partners = (
        (0, p >= 1, -1, 1),
        (1, p < last, 1, 0),
        (1, p < last, 0, 2),
        (2, p < last, 0, 1),
        (2, jnp.logical_and(p >= 1, p < last), -1, 3),
        (2, p >= 1, -1, 2),
        (2, p < last, 1, 2),
        (3, p < last - 1, 1, 2),
        (3, p < last - 1, 2, 3),
        (3, p >= 2, -2, 3),
    )
    for role, meets, shift, chan in partners:

        @pl.when(jnp.logical_and(pair == role, meets))
        def _(shift=shift, chan=chan):
            pl.semaphore_signal(
                barrier, inc=1, device_id={"panel": p + shift, "chan": chan}, device_id_type=MESH
            )

    met = sum(
        jnp.where(jnp.logical_and(pair == role, meets), 1, 0) for role, meets, _, _ in partners
    )

    @pl.when(met > 0)
    def _():
        pl.semaphore_wait(barrier, met)

    coupling_copy.wait()
    size_copy.wait()

    @pl.when(pair == 0)
    def _pair0():
        @pl.when(p >= 1)
        def _():
            each(lambda c: right_copy(0, c, p - 1, 1).start())

        left_copies[0].wait()
        own_copy.wait()
        rows_live, cols_live = live(p), live(p)
        mask_block(own, own, rows_live, cols_live)
        multiply(half_a, left.at[0], own)
        right_copies[0].wait()
        weight = coupling[0, 0, 0]

        def kept(c):
            acc[c] = weight * outer_dot(half_a[...], right[0, pl.ds(pl.multiple_of(c * STEP, STEP), STEP), :])

        each(kept)
        right_copies[1].wait()
        left_copies[1].wait()

        @pl.when(p >= 1)
        def _():
            def fold(c):
                mix_copy(c, p - 1, 1).wait_recv()
                half_b[:, strip(c)] = dot(left[1], in_psi[c]).astype(BF16)

            each(fold)

            def finish(c):
                moved = outer_dot(half_b[...], right[1, strip(c), :])
                write_out(c, acc[c] + moved, rows_live, cols_live)

            each(finish)
            each(lambda c: right_copy(0, c, p - 1, 1).wait_send())

        @pl.when(p == 0)
        def _():
            each(lambda c: write_out(c, acc[c], rows_live, cols_live))

    @pl.when(pair == 1)
    def _pair1():
        left_copies[0].wait()
        own_copy.wait()

        @pl.when(p == last)
        def _():
            write_zeros()

        @pl.when(p < last)
        def _():
            rows_live, cols_live = live(p), live(p + 1)

            def mix(c):
                psi_copy(c, p, 2).wait_recv()
                mine = own[:, strip(c)].astype(jnp.float32)
                theirs = in_psi[c].astype(jnp.float32)
                keep = inside(mine.shape, 0, c * STEP, rows_live, cols_live)

                def blend(x, y):
                    return jnp.where(keep, x * mine + y * theirs, 0.0).astype(BF16)

                mixed[c] = blend(coupling[1, 0, 1], coupling[1, 0, 2])
                mix_copy(c, p + 1, 0).start()
                both[:, :STEP] = blend(coupling[0, 2, 1], coupling[0, 2, 2])
                both[:, STEP:] = blend(coupling[0, 1, 1], coupling[0, 1, 2])
                product = dot(left[0], both[...]).astype(BF16)
                half_b[:, strip(c)] = product[:, :STEP]
                half_a[:, strip(c)] = product[:, STEP:]

            each(mix)

            def kept(c):
                right_copy(0, c, p + 1, 0).wait_recv()
                block = in_right[pl.ds(pl.multiple_of(c * STEP, STEP), STEP), :]
                out_part[c] = outer_dot(half_b[...], block).astype(BF16)
                part_copy(c, p, 2).start()
                acc[c] = outer_dot(half_a[...], block)

            each(kept)

            def finish(c):
                part_copy(c, p, 2).wait_recv()
                moved = coupling[1, 1, 3] * in_part[c].astype(jnp.float32)
                write_out(c, acc[c] + moved, rows_live, cols_live)

            each(finish)
            each(lambda c: mix_copy(c, p + 1, 0).wait_send())
            each(lambda c: part_copy(c, p, 2).wait_send())

    @pl.when(pair == 2)
    def _pair2():
        @pl.when(p < last)
        def _():
            each(lambda c: psi_copy(c, p, 1).start())

        left_copies[1].wait()

        @pl.when(jnp.logical_and(p >= 1, p < last))
        def _():
            each(lambda c: psi_copy(c, p - 1, 3).wait_recv(), early)

        @pl.when(p >= 1)
        def _():
            each(lambda c: right_copy(1, c, p - 1, 2).start())

        @pl.when(p == last)
        def _():
            write_zeros()

        @pl.when(p < last)
        def _():
            rows_live, cols_live = live(p), live(p + 1)

            @pl.when(p >= 1)
            def _():
                def raise_strip(c):
                    @pl.when(c >= early)
                    def _():
                        psi_copy(c, p - 1, 3).wait_recv()

                    block = in_psi[c]
                    keep = inside(block.shape, 0, c * STEP, live(p - 1), live(p + 1))
                    block = jnp.where(keep, block.astype(jnp.float32), 0.0).astype(BF16)
                    half_a[:, strip(c)] = dot(left[1], block).astype(BF16)

                each(raise_strip)

            @pl.when(p == 0)
            def _():
                half_a[...] = jnp.zeros_like(half_a)

            def moved(c):
                right_copy(1, c, p + 1, 2).wait_recv()
                block = in_right[pl.ds(pl.multiple_of(c * STEP, STEP), STEP), :]
                value = outer_dot(half_a[...], block)
                out_part[c] = value.astype(BF16)
                part_copy(c, p, 1).start()
                acc[c] = coupling[1, 2, 3] * value

            each(moved)

            def finish(c):
                part_copy(c, p, 1).wait_recv()
                write_out(c, acc[c] + in_part[c].astype(jnp.float32), rows_live, cols_live)

            each(finish)
            each(lambda c: psi_copy(c, p, 1).wait_send())
            each(lambda c: part_copy(c, p, 1).wait_send())

        @pl.when(p >= 1)
        def _():
            each(lambda c: right_copy(1, c, p - 1, 2).wait_send())

    @pl.when(pair == 3)
    def _pair3():
        @pl.when(p < last - 1)
        def _():
            each(lambda c: psi_copy(c, p + 1, 2).start())

        @pl.when(p >= 2)
        def _():
            each(lambda c: right_copy(0, c, p - 2, 3).start())

        left_copies[0].wait()
        own_copy.wait()

        @pl.when(p >= last - 1)
        def _():
            write_zeros()

        @pl.when(p < last - 1)
        def _():
            rows_live, cols_live = live(p), live(p + 2)
            mask_block(own, own, rows_live, cols_live)
            multiply(half_a, left.at[0], own)

            def kept(c):
                right_copy(0, c, p + 2, 3).wait_recv()
                block = in_right[pl.ds(pl.multiple_of(c * STEP, STEP), STEP), :]
                value = coupling[0, 3, 3] * outer_dot(half_a[...], block)
                write_out(c, value, rows_live, cols_live)

            each(kept)
            each(lambda c: psi_copy(c, p + 1, 2).wait_send())

        @pl.when(p >= 2)
        def _():
            each(lambda c: right_copy(0, c, p - 2, 3).wait_send())


def shards(sectors, wavefunction, left_env, right_env, coupling, sec_size):
    width = wavefunction.shape[-1]
    steps = width // STEP
    square = pltpu.VMEM((width, width), BF16)
    strips = (steps, width, STEP)
    return pl.pallas_call(
        functools.partial(kernel, sectors),
        out_shape=jax.ShapeDtypeStruct(wavefunction.shape, BF16),
        in_specs=[pl.BlockSpec(memory_space=pl.ANY)] * 5,
        out_specs=pl.BlockSpec(memory_space=pltpu.VMEM),
        scratch_shapes=[
            pltpu.VMEM((2, width, width), BF16),
            pltpu.VMEM((2, width, width), BF16),
            square,
            pltpu.VMEM(strips, BF16),
            square,
            pltpu.VMEM(strips, BF16),
            pltpu.VMEM(strips, BF16),
            pltpu.VMEM(strips, BF16),
            pltpu.VMEM((width, 2 * STEP), BF16),
            square,
            square,
            pltpu.VMEM(strips, jnp.float32),
            pltpu.SMEM(coupling.shape, coupling.dtype),
            pltpu.SMEM(sec_size.shape, sec_size.dtype),
            pltpu.SemaphoreType.DMA((7,)),
        ]
        + [pltpu.SemaphoreType.DMA((steps,))] * 6,
        compiler_params=pltpu.CompilerParams(
            collective_id=0, has_side_effects=True, vmem_limit_bytes=56 * 1024 * 1024
        ),
    )(coupling, sec_size, wavefunction, left_env, right_env)


def solution(mesh):
    sectors = mesh.shape["panel"]
    return jax.shard_map(
        functools.partial(shards, sectors),
        mesh=mesh,
        in_specs=(
            P("chan", "panel", None, None),
            P(None, "panel", None, None),
            P(None, "panel", None, None),
            P(),
            P(),
        ),
        out_specs=P("chan", "panel", None, None),
        check_vma=False,
    )
```

```python
import functools

import jax
import jax.numpy as jnp
from jax import lax
from jax.experimental import pallas as pl
from jax.experimental.pallas import tpu as pltpu
from jax.sharding import PartitionSpec as P

MESH = pl.DeviceIdType.MESH
STEP = 128
ROWS = 256
BF16 = jnp.bfloat16


def dot(a, b):
    return jnp.dot(a, b, preferred_element_type=jnp.float32)


def outer_dot(a, b):
    return lax.dot_general(a, b, (((1,), (1,)), ((), ())), preferred_element_type=jnp.float32)


def inside(shape, row0, col0, rows_live, cols_live):
    row = lax.broadcasted_iota(jnp.int32, shape, 0) + row0
    col = lax.broadcasted_iota(jnp.int32, shape, 1) + col0
    return jnp.logical_and(row < rows_live, col < cols_live)


def kernel(
    sectors,
    coupling_hbm,
    sec_size_hbm,
    psi_hbm,
    left_hbm,
    right_hbm,
    out,
    left,
    right,
    own,
    in_psi,
    in_right,
    in_part,
    out_part,
    mixed,
    both,
    half_a,
    half_b,
    acc,
    coupling,
    sec_size,
    local_sem,
    psi_send,
    psi_recv,
    right_send,
    right_recv,
    part_send,
    part_recv,
):
    width = own.shape[0]
    steps = width // STEP
    early = steps - 1
    p = lax.axis_index("panel")
    pair = lax.axis_index("chan")
    last = sectors - 1

    psi_src = psi_hbm.at[0, 0]
    left_copies = [
        pltpu.make_async_copy(left_hbm.at[k, 0], left.at[k], local_sem.at[k]) for k in range(2)
    ]
    right_copies = [
        pltpu.make_async_copy(right_hbm.at[k, 0], right.at[k], local_sem.at[2 + k])
        for k in range(2)
    ]
    own_copy = pltpu.make_async_copy(psi_src, own, local_sem.at[4])
    coupling_copy = pltpu.make_async_copy(coupling_hbm, coupling, local_sem.at[5])
    size_copy = pltpu.make_async_copy(sec_size_hbm, sec_size, local_sem.at[6])
    coupling_copy.start()
    size_copy.start()

    def live(sector):
        exists = jnp.logical_and(sector >= 0, sector < sectors)
        return jnp.where(exists, sec_size[jnp.clip(sector, 0, last)], 0)

    def rows_at(ref, c, n=STEP):
        return ref.at[pl.ds(pl.multiple_of(c * n, n), n), :]

    def remote(src, dst, send, recv, panel, chan):
        return pltpu.make_async_remote_copy(
            src_ref=src,
            dst_ref=dst,
            send_sem=send,
            recv_sem=recv,
            device_id={"panel": panel, "chan": chan},
            device_id_type=MESH,
        )

    def strip(c):
        return pl.ds(pl.multiple_of(c * STEP, STEP), STEP)

    def strip_copy(src, c, panel, chan):
        return remote(src, in_psi.at[c], psi_send.at[c], psi_recv.at[c], panel, chan)

    def psi_copy(c, panel, chan):
        return strip_copy(psi_src.at[:, strip(c)], c, panel, chan)

    def mix_copy(c, panel, chan):
        return strip_copy(mixed.at[c], c, panel, chan)

    def right_copy(k, c, panel, chan):
        src = rows_at(right_hbm.at[k, 0], c)
        return remote(src, rows_at(in_right, c), right_send.at[c], right_recv.at[c], panel, chan)

    def part_copy(c, panel, chan):
        return remote(
            out_part.at[c], in_part.at[c], part_send.at[c], part_recv.at[c], panel, chan
        )

    def each(body, n=None):
        def step(c, carry):
            body(c)
            return carry

        lax.fori_loop(0, steps if n is None else n, step, 0)

    def multiply(dst, a, b):
        def body(r):
            at = pl.ds(pl.multiple_of(r * ROWS, ROWS), ROWS)
            dst[at, :] = dot(a[at, :], b[...]).astype(BF16)

        each(body, width // ROWS)

    def mask_block(dst, src, rows_live, cols_live):
        def body(c):
            at = pl.ds(pl.multiple_of(c * STEP, STEP), STEP)
            block = src[at, :]
            keep = inside(block.shape, c * STEP, 0, rows_live, cols_live)
            dst[at, :] = jnp.where(keep, block.astype(jnp.float32), 0.0).astype(BF16)

        each(body)

    def write_out(c, value, rows_live, cols_live):
        at = pl.ds(pl.multiple_of(c * STEP, STEP), STEP)
        keep = inside(value.shape, 0, c * STEP, rows_live, cols_live)
        out[0, 0, :, at] = jnp.where(keep, value, 0.0).astype(BF16)

    def write_zeros():
        out[...] = jnp.zeros_like(out)

    @pl.when(pair != 2)
    def _():
        left_copies[0].start()
        own_copy.start()

    @pl.when(jnp.logical_or(pair == 0, pair == 2))
    def _():
        left_copies[1].start()

    @pl.when(pair == 0)
    def _():
        right_copies[0].start()
        right_copies[1].start()

    barrier = pltpu.get_barrier_semaphore()
    partners = (
        (0, p >= 1, -1, 1),
        (1, p < last, 1, 0),
        (1, p < last, 0, 2),
        (2, p < last, 0, 1),
        (2, jnp.logical_and(p >= 1, p < last), -1, 3),
        (2, p >= 1, -1, 2),
        (2, p < last, 1, 2),
        (3, p < last - 1, 1, 2),
        (3, p < last - 1, 2, 3),
        (3, p >= 2, -2, 3),
    )
    for role, meets, shift, chan in partners:

        @pl.when(jnp.logical_and(pair == role, meets))
        def _(shift=shift, chan=chan):
            pl.semaphore_signal(
                barrier, inc=1, device_id={"panel": p + shift, "chan": chan}, device_id_type=MESH
            )

    met = sum(
        jnp.where(jnp.logical_and(pair == role, meets), 1, 0) for role, meets, _, _ in partners
    )

    @pl.when(met > 0)
    def _():
        pl.semaphore_wait(barrier, met)

    coupling_copy.wait()
    size_copy.wait()

    @pl.when(pair == 0)
    def _pair0():
        @pl.when(p >= 1)
        def _():
            each(lambda c: right_copy(0, c, p - 1, 1).start())

        left_copies[0].wait()
        own_copy.wait()
        rows_live, cols_live = live(p), live(p)
        mask_block(own, own, rows_live, cols_live)
        multiply(half_a, left.at[0], own)
        right_copies[0].wait()
        weight = coupling[0, 0, 0]

        def kept(c):
            acc[c] = weight * outer_dot(half_a[...], right[0, pl.ds(pl.multiple_of(c * STEP, STEP), STEP), :])

        each(kept)
        right_copies[1].wait()
        left_copies[1].wait()

        @pl.when(p >= 1)
        def _():
            def fold(c):
                mix_copy(c, p - 1, 1).wait_recv()
                half_b[:, strip(c)] = dot(left[1], in_psi[c]).astype(BF16)

            each(fold)

            def finish(c):
                moved = outer_dot(half_b[...], right[1, strip(c), :])
                write_out(c, acc[c] + moved, rows_live, cols_live)

            each(finish)
            each(lambda c: right_copy(0, c, p - 1, 1).wait_send())

        @pl.when(p == 0)
        def _():
            each(lambda c: write_out(c, acc[c], rows_live, cols_live))

    @pl.when(pair == 1)
    def _pair1():
        left_copies[0].wait()
        own_copy.wait()

        @pl.when(p == last)
        def _():
            write_zeros()

        @pl.when(p < last)
        def _():
            rows_live, cols_live = live(p), live(p + 1)

            def mix(c):
                psi_copy(c, p, 2).wait_recv()
                mine = own[:, strip(c)].astype(jnp.float32)
                theirs = in_psi[c].astype(jnp.float32)
                keep = inside(mine.shape, 0, c * STEP, rows_live, cols_live)

                def blend(x, y):
                    return jnp.where(keep, x * mine + y * theirs, 0.0).astype(BF16)

                mixed[c] = blend(coupling[1, 0, 1], coupling[1, 0, 2])
                mix_copy(c, p + 1, 0).start()
                both[:, :STEP] = blend(coupling[0, 2, 1], coupling[0, 2, 2])
                both[:, STEP:] = blend(coupling[0, 1, 1], coupling[0, 1, 2])
                product = dot(left[0], both[...]).astype(BF16)
                half_b[:, strip(c)] = product[:, :STEP]
                half_a[:, strip(c)] = product[:, STEP:]

            each(mix)

            def kept(c):
                right_copy(0, c, p + 1, 0).wait_recv()
                block = in_right[pl.ds(pl.multiple_of(c * STEP, STEP), STEP), :]
                out_part[c] = outer_dot(half_b[...], block).astype(BF16)
                part_copy(c, p, 2).start()
                acc[c] = outer_dot(half_a[...], block)

            each(kept)

            def finish(c):
                part_copy(c, p, 2).wait_recv()
                moved = coupling[1, 1, 3] * in_part[c].astype(jnp.float32)
                write_out(c, acc[c] + moved, rows_live, cols_live)

            each(finish)
            each(lambda c: mix_copy(c, p + 1, 0).wait_send())
            each(lambda c: part_copy(c, p, 2).wait_send())

    @pl.when(pair == 2)
    def _pair2():
        @pl.when(p < last)
        def _():
            each(lambda c: psi_copy(c, p, 1).start())

        left_copies[1].wait()

        @pl.when(jnp.logical_and(p >= 1, p < last))
        def _():
            each(lambda c: psi_copy(c, p - 1, 3).wait_recv(), early)

        @pl.when(p >= 1)
        def _():
            each(lambda c: right_copy(1, c, p - 1, 2).start())

        @pl.when(p == last)
        def _():
            write_zeros()

        @pl.when(p < last)
        def _():
            rows_live, cols_live = live(p), live(p + 1)

            @pl.when(p >= 1)
            def _():
                def raise_strip(c):
                    @pl.when(c >= early)
                    def _():
                        psi_copy(c, p - 1, 3).wait_recv()

                    block = in_psi[c]
                    keep = inside(block.shape, 0, c * STEP, live(p - 1), live(p + 1))
                    block = jnp.where(keep, block.astype(jnp.float32), 0.0).astype(BF16)
                    half_a[:, strip(c)] = dot(left[1], block).astype(BF16)

                each(raise_strip)

            @pl.when(p == 0)
            def _():
                half_a[...] = jnp.zeros_like(half_a)

            def moved(c):
                right_copy(1, c, p + 1, 2).wait_recv()
                block = in_right[pl.ds(pl.multiple_of(c * STEP, STEP), STEP), :]
                value = outer_dot(half_a[...], block)
                out_part[c] = value.astype(BF16)
                part_copy(c, p, 1).start()
                acc[c] = coupling[1, 2, 3] * value

            each(moved)

            def finish(c):
                part_copy(c, p, 1).wait_recv()
                write_out(c, acc[c] + in_part[c].astype(jnp.float32), rows_live, cols_live)

            each(finish)
            each(lambda c: psi_copy(c, p, 1).wait_send())
            each(lambda c: part_copy(c, p, 1).wait_send())

        @pl.when(p >= 1)
        def _():
            each(lambda c: right_copy(1, c, p - 1, 2).wait_send())

    @pl.when(pair == 3)
    def _pair3():
        @pl.when(p < last - 1)
        def _():
            each(lambda c: psi_copy(c, p + 1, 2).start())

        @pl.when(p >= 2)
        def _():
            each(lambda c: right_copy(0, c, p - 2, 3).start())

        left_copies[0].wait()
        own_copy.wait()

        @pl.when(p >= last - 1)
        def _():
            write_zeros()

        @pl.when(p < last - 1)
        def _():
            rows_live, cols_live = live(p), live(p + 2)
            mask_block(own, own, rows_live, cols_live)
            multiply(half_a, left.at[0], own)

            def kept(c):
                right_copy(0, c, p + 2, 3).wait_recv()
                block = in_right[pl.ds(pl.multiple_of(c * STEP, STEP), STEP), :]
                value = coupling[0, 3, 3] * outer_dot(half_a[...], block)
                write_out(c, value, rows_live, cols_live)

            each(kept)
            each(lambda c: psi_copy(c, p + 1, 2).wait_send())

        @pl.when(p >= 2)
        def _():
            each(lambda c: right_copy(0, c, p - 2, 3).wait_send())


def shards(sectors, wavefunction, left_env, right_env, coupling, sec_size):
    width = wavefunction.shape[-1]
    steps = width // STEP
    square = pltpu.VMEM((width, width), BF16)
    strips = (steps, width, STEP)
    return pl.pallas_call(
        functools.partial(kernel, sectors),
        out_shape=jax.ShapeDtypeStruct(wavefunction.shape, BF16),
        in_specs=[pl.BlockSpec(memory_space=pl.ANY)] * 5,
        out_specs=pl.BlockSpec(memory_space=pltpu.VMEM),
        scratch_shapes=[
            pltpu.VMEM((2, width, width), BF16),
            pltpu.VMEM((2, width, width), BF16),
            square,
            pltpu.VMEM(strips, BF16),
            square,
            pltpu.VMEM(strips, BF16),
            pltpu.VMEM(strips, BF16),
            pltpu.VMEM(strips, BF16),
            pltpu.VMEM((width, 2 * STEP), BF16),
            square,
            square,
            pltpu.VMEM(strips, jnp.float32),
            pltpu.SMEM(coupling.shape, coupling.dtype),
            pltpu.SMEM(sec_size.shape, sec_size.dtype),
            pltpu.SemaphoreType.DMA((7,)),
        ]
        + [pltpu.SemaphoreType.DMA((steps,))] * 6,
        compiler_params=pltpu.CompilerParams(
            collective_id=0, has_side_effects=True, vmem_limit_bytes=56 * 1024 * 1024
        ),
    )(coupling, sec_size, wavefunction, left_env, right_env)


def solution(mesh):
    sectors = mesh.shape["panel"]
    return jax.shard_map(
        functools.partial(shards, sectors),
        mesh=mesh,
        in_specs=(
            P("chan", "panel", None, None),
            P(None, "panel", None, None),
            P(None, "panel", None, None),
            P(),
            P(),
        ),
        out_specs=P("chan", "panel", None, None),
        check_vma=False,
    )
```
